128 devices in a mesh: pop: 4 (over y_hi, core), tp: 16 (over z, x), pp: 2 (over y_lo).
Axes of the slice: x: 4, y: 4 (y_hi: 2, y_lo: 2; y = y_hi * 2 + y_lo), z: 4, core: 2. Of those that a mesh axis runs over, the one named last changes fastest.
Arguments:
- hidden_in: bfloat16 [256, 8, 4096], P('tp', 'pop'), may hold values from -6 to 6
- norm_gain: float32 [2, 4096], P('pp'), may hold values from 0.5 to 1.5
- w_gate: bfloat16 [2, 4096, 12288], P('pp', None, 'tp'), may hold values from -0.09375 to 0.09375
- w_up: bfloat16 [2, 4096, 12288], P('pp', None, 'tp'), may hold values from -0.09375 to 0.09375
- w_down: bfloat16 [2, 12288, 4096], P('pp', 'tp'), may hold values from -0.0546875 to 0.0546875
- gate_left: bfloat16 [2, 8, 4096], P('pp', 'pop'), may hold values from -6 to 6
- gate_right: bfloat16 [2, 8, 12288], P('pp', 'pop', 'tp'), may hold values from -6 to 6
- up_left: bfloat16 [2, 8, 4096], P('pp', 'pop'), may hold values from -6 to 6
- up_right: bfloat16 [2, 8, 12288], P('pp', 'pop', 'tp'), may hold values from -6 to 6
- down_left: bfloat16 [2, 8, 12288], P('pp', 'pop', 'tp'), may hold values from -6 to 6
- down_right: bfloat16 [2, 8, 4096], P('pp', 'pop'), may hold values from -6 to 6
- ranks: int32 [8], P('pop'), may hold values from 0 to 7, each once
Outputs:
- section_out: bfloat16 [2, 256, 8, 4096], P('pp', 'tp', 'pop')
- update_gate: bfloat16 [2, 4096, 12288], P('pp', 'pop', 'tp')
- update_up: bfloat16 [2, 4096, 12288], P('pp', 'pop', 'tp')
- update_down: bfloat16 [2, 12288, 4096], P('pp', 'tp', 'pop')
The draws below stay inside these ranges and needn't reach their ends.
Inputs may be any that keep to these rules, and one draw needn't show every extreme that they name: `ranks`: each number from 0 to 7 is the rank of exactly one member.
All inputs are finite; a program needn't handle non-finite values.
Results may differ from the reference program's by a relative error of at most 0.014.
Values may be sent and summed in bfloat16 or wider, within the bound.
No kernel may reach another device: no remote copies, remote signals or barrier semaphores. Data moves between devices by JAX's collectives and lax.ppermute only.
A program may use at most 128 MiB of HBM per device.

```python
import math
import jax
import jax.numpy as jnp
from jax import lax

D = 4096
FF = 12288
SEQ = 256
MEM_DEV = 2
POP = 8
SECTIONS = 2
N_POP = 4


def shard_levels(key, shape, split, low, high):
    loudness, own = 1.0, jax.random.fold_in(key, 6)
    for axis_at, parts in split:
        draws = jnp.exp(jax.random.uniform(jax.random.fold_in(own, axis_at), (parts,), jnp.float32, low / len(split), high / len(split)))
        loudness = loudness * jnp.repeat(draws, shape[axis_at] // parts).reshape([-1 if axis == axis_at else 1 for axis in range(len(shape))])
    return loudness


def normal_values(rng, shape, deviation, most, pieces=(), held_as=jnp.bfloat16):
    array = jax.random.normal(rng, shape, jnp.float32) * deviation
    if len(pieces) > 0:
        array = shard_levels(rng, shape, pieces, -0.22, 0.18) * array
    return jnp.clip(array, min=-most, max=most).astype(held_as)


def setup_inputs(seed: int = 0) -> dict:
    streams_of = jax.random.split(jax.random.key(seed), 13)
    hidden_in = normal_values(streams_of[0], (SEQ, POP, D), 1.0, 6.0, ((0, 16), (1, 4)))
    norm_gain = jnp.clip(1.0 + 0.1 * jax.random.normal(streams_of[1], (SECTIONS, D), jnp.float32), 0.5, 1.5)
    w_gate = normal_values(streams_of[2], (SECTIONS, D, FF), D ** -0.5, 0.09375, ((0, 2), (2, 16)))
    w_up = normal_values(streams_of[3], (SECTIONS, D, FF), D ** -0.5, 0.09375, ((0, 2), (2, 16)))
    w_down = normal_values(streams_of[4], (SECTIONS, FF, D), FF ** -0.5, 0.0546875, ((0, 2), (1, 16)))
    gate_left = normal_values(streams_of[5], (SECTIONS, POP, D), 1.0, 6.0, ((0, 2), (1, 4)))
    gate_right = normal_values(streams_of[6], (SECTIONS, POP, FF), 1.0, 6.0, ((0, 2), (1, 4), (2, 16)))
    up_left = normal_values(streams_of[7], (SECTIONS, POP, D), 1.0, 6.0, ((0, 2), (1, 4)))
    up_right = normal_values(streams_of[8], (SECTIONS, POP, FF), 1.0, 6.0, ((0, 2), (1, 4), (2, 16)))
    down_left = normal_values(streams_of[9], (SECTIONS, POP, FF), 1.0, 6.0, ((0, 2), (1, 4), (2, 16)))
    down_right = normal_values(streams_of[10], (SECTIONS, POP, D), 1.0, 6.0, ((0, 2), (1, 4)))
    ranks = jax.random.permutation(streams_of[11], POP).astype(jnp.int32)
    return {"hidden_in": hidden_in, "norm_gain": norm_gain, "w_gate": w_gate, "w_up": w_up, "w_down": w_down, "gate_left": gate_left, "gate_right": gate_right, "up_left": up_left, "up_right": up_right, "down_left": down_left, "down_right": down_right, "ranks": ranks}


sigma_scale = 0.3
norm_eps = 1e-05

def section_layer(hidden, gain, w_gate, w_up, w_down, gate_left, gate_right, up_left, up_right, down_left, down_right):
    values = hidden.astype(jnp.float32)
    mean_sq = lax.optimization_barrier(jnp.mean(values * values, axis=-1, keepdims=True))
    normed = (values * lax.rsqrt(mean_sq + norm_eps) * gain).astype(jnp.bfloat16)
    flat = normed.reshape(SEQ * POP, D)
    normed_wide = normed.astype(jnp.float32)
    coef_in = sigma_scale / math.sqrt(D)
    coef_hidden = sigma_scale / math.sqrt(FF)
    gate = jnp.dot(flat, w_gate, preferred_element_type=jnp.float32).reshape(SEQ, POP, FF)
    gate_side = jnp.einsum('spd,pd->sp', normed_wide, gate_left.astype(jnp.float32))
    gate = gate + coef_in * gate_side[:, :, None] * gate_right.astype(jnp.float32)[None]
    upper = jnp.dot(flat, w_up, preferred_element_type=jnp.float32).reshape(SEQ, POP, FF)
    up_side = jnp.einsum('spd,pd->sp', normed_wide, up_left.astype(jnp.float32))
    upper = upper + coef_in * up_side[:, :, None] * up_right.astype(jnp.float32)[None]
    inner = (jax.nn.silu(gate) * upper).astype(jnp.bfloat16)
    term = jnp.dot(inner.reshape(SEQ * POP, FF), w_down, preferred_element_type=jnp.float32).reshape(SEQ, POP, D)
    down_side = jnp.einsum('spf,pf->sp', inner.astype(jnp.float32), down_left.astype(jnp.float32))
    term = term + coef_hidden * down_side[:, :, None] * down_right.astype(jnp.float32)[None]
    return (values + term).astype(jnp.bfloat16)

def grouped_outer(fitness, left, right):
    total = jnp.zeros((left.shape[1], right.shape[1]), jnp.float32)
    for group in range(N_POP):
        lower = group * MEM_DEV
        weighted = fitness[lower:lower + MEM_DEV, None] * left[lower:lower + MEM_DEV].astype(jnp.float32)
        part = jnp.dot(weighted.T, right[lower:lower + MEM_DEV].astype(jnp.float32), precision=lax.Precision.HIGHEST)
        total = total + lax.optimization_barrier(part.astype(jnp.bfloat16)).astype(jnp.float32)
    return total.astype(jnp.bfloat16)

def reference(hidden_in, norm_gain, w_gate, w_up, w_down, gate_left, gate_right, up_left, up_right, down_left, down_right, ranks):
    current = hidden_in
    outputs = []
    for section in range(SECTIONS):
        current = section_layer(current, norm_gain[section], w_gate[section], w_up[section], w_down[section], gate_left[section], gate_right[section], up_left[section], up_right[section], down_left[section], down_right[section])
        outputs.append(current)
    section_out = jnp.stack(outputs)
    fitness = (2.0 * ranks.astype(jnp.float32) / (POP - 1) - 1.0) / math.sqrt(POP)
    update_gate = jnp.stack([grouped_outer(fitness, gate_left[section], gate_right[section]) for section in range(SECTIONS)])
    update_up = jnp.stack([grouped_outer(fitness, up_left[section], up_right[section]) for section in range(SECTIONS)])
    update_down = jnp.stack([grouped_outer(fitness, down_left[section], down_right[section]) for section in range(SECTIONS)])
    return (section_out, update_gate, update_up, update_down)
```

```python
import math

import jax
import jax.numpy as jnp
from jax import lax
from jax.experimental import pallas as pl
from jax.experimental.pallas import tpu as pltpu
from jax.sharding import PartitionSpec as P

sigma_scale = 0.3
norm_eps = 1e-05
SIDE = 4


def plane_route(level, shift):
    pairs = []
    for pop in range(4):
        for z in range(SIDE):
            for x in range(SIDE):
                along_x = (pop % 2 == 0) == (level == "near")
                nz, nx = (z, (x + shift) % SIDE) if along_x else ((z + shift) % SIDE, x)
                pairs.append((pop * 16 + z * SIDE + x, pop * 16 + nz * SIDE + nx))
    return pairs


def plane_send(block, level, shift):
    return lax.ppermute(block, ("pop", "tp"), plane_route(level, shift))


def feed_forward(rows, w_gate, w_up, w_down, gate_left, gate_wide, up_left, up_wide, down_left, down_wide):
    gate = jnp.einsum("bkrd,df->bkrf", rows, w_gate, preferred_element_type=jnp.float32)
    gate_side = jnp.einsum("bkrd,kd->bkr", rows, gate_left, preferred_element_type=jnp.float32)
    gate = gate + gate_side[..., None] * gate_wide
    upper = jnp.einsum("bkrd,df->bkrf", rows, w_up, preferred_element_type=jnp.float32)
    up_side = jnp.einsum("bkrd,kd->bkr", rows, up_left, preferred_element_type=jnp.float32)
    upper = upper + up_side[..., None] * up_wide
    inner = (jax.nn.silu(gate) * upper).astype(jnp.bfloat16)
    term = jnp.einsum("bkrf,fd->bkrd", inner, w_down, preferred_element_type=jnp.float32)
    down_side = jnp.einsum("bkrf,kf->bkr", inner, down_left, preferred_element_type=jnp.float32)
    return (term + down_side[..., None] * down_wide).astype(jnp.bfloat16)


def plus(a, b):
    return (a.astype(jnp.float32) + b.astype(jnp.float32)).astype(jnp.bfloat16)


def section(block, gain, layer):
    values = block.astype(jnp.float32)
    mean_sq = jnp.mean(values * values, axis=-1, keepdims=True)
    normed = (values * lax.rsqrt(mean_sq + norm_eps) * gain).astype(jnp.bfloat16)
    near = [normed] + [plane_send(normed, "near", s) for s in (1, -1, 2)]
    own = jnp.stack(near)
    left = plane_send(own, "far", 1)
    right = plane_send(own, "far", -1)
    far_a = plane_send(left[:2], "far", 1)
    far_b = plane_send(right[2:], "far", -1)
    far = jnp.concatenate([far_a, far_b])
    t_own = layer(own)
    t_left = layer(left)
    t_right = layer(right)
    t_far = layer(far)
    from_left = plane_send(t_far[:2], "far", 1)
    from_right = plane_send(t_far[2:], "far", -1)
    to_right = jnp.concatenate([plus(t_right[:2], from_left), t_right[2:]])
    to_left = jnp.concatenate([t_left[:2], plus(t_left[2:], from_right)])
    got_left = plane_send(to_right, "far", 1)
    got_right = plane_send(to_left, "far", -1)
    total = t_own.astype(jnp.float32) + got_left.astype(jnp.float32) + got_right.astype(jnp.float32)
    sent = total.astype(jnp.bfloat16)
    parts = [plane_send(sent[2], "near", 1), plane_send(sent[1], "near", -1), plane_send(sent[3], "near", 2)]
    summed = total[0] + sum(p.astype(jnp.float32) for p in parts)
    return (values + summed).astype(jnp.bfloat16)


def outer_kernel(left_ref, right_ref, out_ref):
    total = None
    for group in range(4):
        part = None
        for m in (2 * group, 2 * group + 1):
            term = left_ref[:, m : m + 1] * right_ref[m : m + 1, :]
            part = term if part is None else part + term
        part = part.astype(jnp.bfloat16).astype(jnp.float32)
        total = part if total is None else total + part
    out_ref[...] = total.astype(jnp.bfloat16)


def grouped_outer(fitness, left, right, tile):
    weighted = (fitness[:, None] * left.astype(jnp.float32)).T
    other = right.astype(jnp.float32)
    rows, cols = weighted.shape[0], other.shape[1]
    return pl.pallas_call(
        outer_kernel,
        grid=(rows // tile,),
        in_specs=[pl.BlockSpec((tile, 8), lambda i: (i, 0)), pl.BlockSpec((8, cols), lambda i: (0, 0))],
        out_specs=pl.BlockSpec((tile, cols), lambda i: (i, 0)),
        out_shape=jax.ShapeDtypeStruct((rows, cols), jnp.bfloat16),
        cost_estimate=pl.CostEstimate(flops=30 * rows * cols, bytes_accessed=2 * rows * cols, transcendentals=0),
    )(weighted, other)


def per_device(hidden_in, norm_gain, w_gate, w_up, w_down, gate_left, gate_right, up_left, up_right, down_left, down_right, ranks):
    members, width = hidden_in.shape[1:]
    section_index = lax.axis_index("pp")
    pop_index = lax.axis_index("pop")
    pops = lax.axis_size("pop")
    population = members * pops
    coef_in = sigma_scale / math.sqrt(width)
    coef_hidden = sigma_scale / math.sqrt(w_gate.shape[-1] * lax.axis_size("tp"))

    vectors = [gate_left[0], gate_right[0], up_left[0], up_right[0], down_left[0], down_right[0]]
    rank_columns = jnp.broadcast_to(ranks.astype(jnp.bfloat16)[:, None], (members, 128))
    packed = jnp.concatenate(vectors + [rank_columns], axis=1)
    everyone = [packed] + [lax.ppermute(packed, "pop", [(i, (i + s) % pops) for i in range(pops)]) for s in (1, 2, 3)]

    def wide(vector, coef):
        return (coef * vector[0].astype(jnp.float32))[None, :, None, :]

    gate_wide, up_wide, down_wide = wide(gate_right, coef_in), wide(up_right, coef_in), wide(down_right, coef_hidden)

    def layer(rows):
        return feed_forward(
            rows, w_gate[0], w_up[0], w_down[0], gate_left[0], gate_wide, up_left[0], up_wide, down_left[0], down_wide
        )

    first_in = hidden_in.transpose(1, 0, 2)
    first = section(first_in, norm_gain[0], layer)
    arrived = lax.ppermute(first, "pp", [(0, 1)])
    second = section(arrived, norm_gain[0], layer)
    output = jnp.where(section_index == 0, first, second).transpose(1, 0, 2)

    everyone = jnp.concatenate(everyone, axis=0)
    all_vectors, at = [], 0
    for vector in vectors:
        all_vectors.append(everyone[:, at : at + vector.shape[1]])
        at += vector.shape[1]
    all_gl, all_gr, all_ul, all_ur, all_dl, all_dr = all_vectors
    fitness = (2.0 * everyone[:, at].astype(jnp.float32) / (population - 1) - 1.0) / math.sqrt(population)
    share = width // pops

    def mine(vector):
        return lax.dynamic_slice_in_dim(vector, pop_index * share, share, 1)

    update_gate = grouped_outer(fitness, mine(all_gl), all_gr, 256)
    update_up = grouped_outer(fitness, mine(all_ul), all_ur, 256)
    update_down = grouped_outer(fitness, all_dl, mine(all_dr), 256)
    return (output[None], update_gate[None], update_up[None], update_down[None])


def solution(mesh):
    placed = (
        P("tp", "pop", None),
        P("pp", None),
        P("pp", None, "tp"),
        P("pp", None, "tp"),
        P("pp", "tp", None),
        P("pp", "pop", None),
        P("pp", "pop", "tp"),
        P("pp", "pop", None),
        P("pp", "pop", "tp"),
        P("pp", "pop", "tp"),
        P("pp", "pop", None),
        P("pop"),
    )
    return jax.shard_map(
        per_device,
        mesh=mesh,
        in_specs=placed,
        out_specs=(
            P("pp", "tp", "pop", None),
            P("pp", "pop", "tp"),
            P("pp", "pop", "tp"),
            P("pp", "tp", "pop"),
        ),
        check_vma=False,
    )
```

```python
import functools
import math

import jax
import jax.numpy as jnp
from jax import lax
from jax.experimental import pallas as pl
from jax.experimental.pallas import tpu as pltpu
from jax.sharding import PartitionSpec as P

sigma_scale = 0.3
norm_eps = 1e-05
SIDE = 4
TILE = 256
DOWN_TILE = 1024
FFN_MIB = 16


def plane_route(level, shift):
    pairs = []
    for pop in range(4):
        for z in range(SIDE):
            for x in range(SIDE):
                along_x = (pop % 2 == 0) == (level == "near")
                nz, nx = (z, (x + shift) % SIDE) if along_x else ((z + shift) % SIDE, x)
                pairs.append((pop * 16 + z * SIDE + x, pop * 16 + nz * SIDE + nx))
    return pairs


def plane_send(block, level, shift):
    return lax.ppermute(block, ("pop", "tp"), plane_route(level, shift))


def ffn_kernel(*refs, blocks):
    pieces, refs = refs[:blocks], refs[blocks:]
    w_gate, w_up, w_down, lefts, gate_right, up_right, down_left, down_right = refs[:8]
    outs, (x_ref, h_ref) = refs[8 : 8 + blocks], refs[8 + blocks :]
    rows = x_ref.shape[0]
    width, hidden = w_gate.shape
    at = 0
    for piece in pieces:
        flat = piece[...].reshape(-1, width)
        x_ref[at : at + flat.shape[0], :] = flat
        at += flat.shape[0]
    member = (lax.broadcasted_iota(jnp.int32, (rows, 1), 0) // 16) % 2
    coef_in = sigma_scale / math.sqrt(width)
    coef_hidden = sigma_scale / math.sqrt(hidden * 16)

    def ranked(sides, at, right, coef):
        first = jnp.where(member == 0, sides[:, at : at + 1] * coef, 0.0)
        second = jnp.where(member == 0, 0.0, sides[:, at + 1 : at + 2] * coef)
        right = right.astype(jnp.float32)
        return first * right[0:1] + second * right[1:2]

    sides = jnp.dot(x_ref[...], lefts[...], preferred_element_type=jnp.float32)
    for step in range(hidden // TILE):
        cols = slice(step * TILE, (step + 1) * TILE)
        gate = jnp.dot(x_ref[...], w_gate[:, cols], preferred_element_type=jnp.float32)
        gate = gate + ranked(sides, 0, gate_right[:, cols], coef_in)
        upper = jnp.dot(x_ref[...], w_up[:, cols], preferred_element_type=jnp.float32)
        upper = upper + ranked(sides, 2, up_right[:, cols], coef_in)
        h_ref[:, cols] = (gate / (1.0 + jnp.exp(-gate)) * upper).astype(jnp.bfloat16)
    downs = jnp.dot(h_ref[...], down_left[...], preferred_element_type=jnp.float32)
    for step in range(width // DOWN_TILE):
        cols = slice(step * DOWN_TILE, (step + 1) * DOWN_TILE)
        term = jnp.dot(h_ref[...], w_down[:, cols], preferred_element_type=jnp.float32)
        term = (term + ranked(downs, 0, down_right[:, cols], coef_hidden)).astype(jnp.bfloat16)
        at = 0
        for out in outs:
            size = out.shape[0] * 32
            out[:, :, :, cols] = term[at : at + size].reshape(out.shape[:3] + (DOWN_TILE,))
            at += size


def feed_forward(pieces, layer):
    rows = sum(p.size for p in pieces) // pieces[0].shape[-1]
    width, hidden = layer[0].shape
    vmem = pl.BlockSpec(memory_space=pltpu.VMEM)
    return pl.pallas_call(
        functools.partial(ffn_kernel, blocks=len(pieces)),
        in_specs=[vmem] * (len(pieces) + len(layer)),
        out_specs=[vmem] * len(pieces),
        out_shape=[jax.ShapeDtypeStruct(p.shape, jnp.bfloat16) for p in pieces],
        scratch_shapes=[pltpu.VMEM((rows, width), jnp.bfloat16), pltpu.VMEM((rows, hidden), jnp.bfloat16)],
        compiler_params=pltpu.CompilerParams(vmem_limit_bytes=FFN_MIB * 1024 * 1024),
        cost_estimate=pl.CostEstimate(flops=6 * rows * width * hidden, bytes_accessed=6 * width * hidden, transcendentals=rows * hidden),
    )(*pieces, *layer)


def section(block, gain, layer, inside_gather=None, inside_scatter=None, first=False):
    values = block.astype(jnp.float32)
    mean_sq = jnp.mean(values * values, axis=-1, keepdims=True)
    normed = (values * lax.rsqrt(mean_sq + norm_eps) * gain).astype(jnp.bfloat16)
    own = jnp.stack([normed] + [plane_send(normed, "near", s) for s in (1, -1, 2)])
    if first:
        own, *layer = lax.optimization_barrier((own, *layer))
    left = plane_send(own, "far", 1)
    right = plane_send(own, "far", -1)
    (t_own,) = feed_forward([own], layer)
    held = ()
    if inside_gather is not None:
        own, *operands = lax.optimization_barrier((own, *inside_gather[1]))
        held = inside_gather[0](*operands)
    left, right, t_own, *held = lax.optimization_barrier((left, right, t_own, *held))
    far = jnp.concatenate([plane_send(left[:2], "far", 1), plane_send(right[2:], "far", -1)])
    t_left, t_right = feed_forward([left, right], layer)
    t_left, t_right, far = lax.optimization_barrier((t_left, t_right, far))
    got = [plane_send(t_right, "far", 1), plane_send(t_left, "far", -1)]
    (t_far,) = feed_forward([far], layer)
    got.append(plane_send(t_far, "far", 2))
    extra = None
    if inside_scatter is not None:
        work, operands = inside_scatter
        t_far, *operands = lax.optimization_barrier((t_far, *(held if operands is None else operands)))
        extra = work(*operands)
        *got, extra = lax.optimization_barrier((*got, extra))
    total = t_own.astype(jnp.float32) + sum(g.astype(jnp.float32) for g in got)
    sent = total.astype(jnp.bfloat16)
    parts = [plane_send(sent[3], "near", 2), plane_send(sent[2], "near", 1), plane_send(sent[1], "near", -1)]
    summed = total[0] + sum(p.astype(jnp.float32) for p in parts)
    return (values + summed).astype(jnp.bfloat16), held, layer, extra


def pack_kernel(*refs):
    out_ref, at = refs[-1], 0
    for ref in refs[:-1]:
        out_ref[:, at : at + ref.shape[-1]] = ref[...].reshape(2, ref.shape[-1])
        at += ref.shape[-1]


def pack(arrays):
    return pl.pallas_call(
        pack_kernel,
        out_shape=jax.ShapeDtypeStruct((2, sum(a.shape[-1] for a in arrays)), jnp.bfloat16),
        compiler_params=pltpu.CompilerParams(vmem_limit_bytes=2 * 1024 * 1024),
    )(*arrays)


def outer_kernel(*refs, spans, share, tile):
    groups, outs = refs[:4], refs[4:]
    step = pl.program_id(0)
    mine = lax.axis_index("pop") * share
    ranks_at = groups[0].shape[1] - 128
    fitness = [(2.0 * g[:, ranks_at : ranks_at + 1].astype(jnp.float32) / 7 - 1.0) / math.sqrt(8) for g in groups]
    for out, (left_at, left_mine, right_at, right_mine) in zip(outs, spans):
        left_cols = pl.ds(pl.multiple_of(left_at + step * tile + (mine if left_mine else 0), 128), tile)
        right_cols = pl.ds(pl.multiple_of(right_at + mine, 128) if right_mine else right_at, out.shape[1])
        total = None
        for group, fit in zip(groups, fitness):
            weighted = (group[:, left_cols].astype(jnp.float32) * fit).T
            right = group[:, right_cols].astype(jnp.float32)
            part = weighted[:, 0:1] * right[0:1] + weighted[:, 1:2] * right[1:2]
            part = part.astype(jnp.bfloat16).astype(jnp.float32)
            total = part if total is None else total + part
        out[...] = total.astype(jnp.bfloat16)


def grouped_outers(groups, spans, share, shape, tile=256):
    rows, cols = shape
    return pl.pallas_call(
        functools.partial(outer_kernel, spans=spans, share=share, tile=tile),
        grid=(rows // tile,),
        in_specs=[pl.BlockSpec(memory_space=pltpu.VMEM)] * 4,
        out_specs=[pl.BlockSpec((tile, cols), lambda i: (i, 0))] * len(spans),
        out_shape=[jax.ShapeDtypeStruct(shape, jnp.bfloat16)] * len(spans),
        compiler_params=pltpu.CompilerParams(vmem_limit_bytes=8 * 1024 * 1024),
        cost_estimate=pl.CostEstimate(
            flops=30 * rows * cols * len(spans), bytes_accessed=2 * rows * cols * len(spans), transcendentals=0
        ),
    )(*groups)


def per_device(hidden_in, norm_gain, w_gate, w_up, w_down, gate_left, gate_right, up_left, up_right, down_left, down_right, ranks):
    members, width = hidden_in.shape[1:]
    section_index = lax.axis_index("pp")
    pops = lax.axis_size("pop")
    vectors = [gate_left[0], gate_right[0], up_left[0], up_right[0], down_left[0], down_right[0]]
    rank_columns = jnp.broadcast_to(ranks.astype(jnp.bfloat16)[:, None], (members, 128))

    def exchange(*arrays):
        packed = pack(arrays)
        return [packed] + [lax.ppermute(packed, "pop", [(i, (i + s) % pops) for i in range(pops)]) for s in (1, 2, 3)]

    lefts = jnp.pad(jnp.concatenate([gate_left[0], up_left[0]]).T, ((0, 0), (0, 124)))
    down_lefts = jnp.pad(down_left[0].T, ((0, 0), (0, 126)))
    layer = (w_gate[0], w_up[0], w_down[0], lefts, gate_right[0], up_right[0], down_lefts, down_right[0])

    share, hidden = width // pops, w_gate.shape[-1]
    starts = [0, width, width + hidden, 2 * width + hidden, 2 * (width + hidden), 2 * width + 3 * hidden]
    gl, gr, ul, ur, dl, dr = starts

    def first_updates(*everyone):
        return grouped_outers(everyone, ((gl, True, gr, False), (ul, True, ur, False)), share, (share, hidden))

    def second_updates(*everyone):
        return grouped_outers(everyone, ((dl, False, dr, True),), share, (hidden, share))

    first_in = hidden_in.transpose(1, 0, 2)
    first, everyone, layer, (update_gate, update_up) = section(
        first_in, norm_gain[0], layer, (exchange, vectors + [rank_columns]), (first_updates, None), True
    )
    arrived = lax.ppermute(first, "pp", [(0, 1)])
    second, _, _, (update_down,) = section(arrived, norm_gain[0], layer, None, (second_updates, everyone))
    output = jnp.where(section_index == 0, first, second).transpose(1, 0, 2)
    return (output[None], update_gate[None], update_up[None], update_down[None])


def solution(mesh):
    placed = (
        P("tp", "pop", None),
        P("pp", None),
        P("pp", None, "tp"),
        P("pp", None, "tp"),
        P("pp", "tp", None),
        P("pp", "pop", None),
        P("pp", "pop", "tp"),
        P("pp", "pop", None),
        P("pp", "pop", "tp"),
        P("pp", "pop", "tp"),
        P("pp", "pop", None),
        P("pop"),
    )
    return jax.shard_map(
        per_device,
        mesh=mesh,
        in_specs=placed,
        out_specs=(
            P("pp", "tp", "pop", None),
            P("pp", "pop", "tp"),
            P("pp", "pop", "tp"),
            P("pp", "tp", "pop"),
        ),
        check_vma=False,
    )
```

```python
import functools
import math

import jax
import jax.numpy as jnp
from jax import lax
from jax.experimental import pallas as pl
from jax.experimental.pallas import tpu as pltpu
from jax.sharding import PartitionSpec as P

sigma_scale = 0.3
norm_eps = 1e-05
SIDE = 4
UPDATE_FLOPS = 1000
TILE = 256
DOWN_TILE = 1024
FFN_MIB = 16


def plane_route(level, shift):
    pairs = []
    for pop in range(4):
        for z in range(SIDE):
            for x in range(SIDE):
                along_x = (pop % 2 == 0) == (level == "near")
                nz, nx = (z, (x + shift) % SIDE) if along_x else ((z + shift) % SIDE, x)
                pairs.append((pop * 16 + z * SIDE + x, pop * 16 + nz * SIDE + nx))
    return pairs


def plane_send(block, level, shift):
    return lax.ppermute(block, ("pop", "tp"), plane_route(level, shift))


def ffn_kernel(*refs, blocks):
    pieces, refs = refs[:blocks], refs[blocks:]
    w_gate, w_up, w_down, lefts, gate_right, up_right, down_left, down_right = refs[:8]
    outs, (x_ref, h_ref) = refs[8 : 8 + blocks], refs[8 + blocks :]
    rows = x_ref.shape[0]
    width, hidden = w_gate.shape
    at = 0
    for piece in pieces:
        flat = piece[...].reshape(-1, width)
        x_ref[at : at + flat.shape[0], :] = flat
        at += flat.shape[0]
    member = (lax.broadcasted_iota(jnp.int32, (rows, 1), 0) // 16) % 2
    coef_in = sigma_scale / math.sqrt(width)
    coef_hidden = sigma_scale / math.sqrt(hidden * 16)

    def ranked(sides, at, right, coef):
        first = jnp.where(member == 0, sides[:, at : at + 1] * coef, 0.0)
        second = jnp.where(member == 0, 0.0, sides[:, at + 1 : at + 2] * coef)
        right = right.astype(jnp.float32)
        return first * right[0:1] + second * right[1:2]

    sides = jnp.dot(x_ref[...], lefts[...], preferred_element_type=jnp.float32)
    for step in range(hidden // TILE):
        cols = slice(step * TILE, (step + 1) * TILE)
        gate = jnp.dot(x_ref[...], w_gate[:, cols], preferred_element_type=jnp.float32)
        gate = gate + ranked(sides, 0, gate_right[:, cols], coef_in)
        upper = jnp.dot(x_ref[...], w_up[:, cols], preferred_element_type=jnp.float32)
        upper = upper + ranked(sides, 2, up_right[:, cols], coef_in)
        h_ref[:, cols] = (gate / (1.0 + jnp.exp(-gate)) * upper).astype(jnp.bfloat16)
    across = (((1,), (1,)), ((), ()))
    downs = lax.dot_general(h_ref[...], down_left[...], across, preferred_element_type=jnp.float32)
    for step in range(width // DOWN_TILE):
        cols = slice(step * DOWN_TILE, (step + 1) * DOWN_TILE)
        term = jnp.dot(h_ref[...], w_down[:, cols], preferred_element_type=jnp.float32)
        term = (term + ranked(downs, 0, down_right[:, cols], coef_hidden)).astype(jnp.bfloat16)
        at = 0
        for out in outs:
            size = out.shape[0] * 32
            out[:, :, :, cols] = term[at : at + size].reshape(out.shape[:3] + (DOWN_TILE,))
            at += size


def feed_forward(pieces, layer):
    rows = sum(p.size for p in pieces) // pieces[0].shape[-1]
    width, hidden = layer[0].shape
    vmem = pl.BlockSpec(memory_space=pltpu.VMEM)
    return pl.pallas_call(
        functools.partial(ffn_kernel, blocks=len(pieces)),
        in_specs=[vmem] * (len(pieces) + len(layer)),
        out_specs=[vmem] * len(pieces),
        out_shape=[jax.ShapeDtypeStruct(p.shape, jnp.bfloat16) for p in pieces],
        scratch_shapes=[pltpu.VMEM((rows, width), jnp.bfloat16), pltpu.VMEM((rows, hidden), jnp.bfloat16)],
        compiler_params=pltpu.CompilerParams(vmem_limit_bytes=FFN_MIB * 1024 * 1024),
        cost_estimate=pl.CostEstimate(flops=6 * rows * width * hidden, bytes_accessed=6 * width * hidden, transcendentals=rows * hidden),
    )(*pieces, *layer)


def section(block, gain, layer, inside_scatter, first=False):
    values = block.astype(jnp.float32)
    mean_sq = jnp.mean(values * values, axis=-1, keepdims=True)
    normed = (values * lax.rsqrt(mean_sq + norm_eps) * gain).astype(jnp.bfloat16)
    own = jnp.stack([normed] + [plane_send(normed, "near", s) for s in (2, 1, -1)])
    if first:
        own, *layer = lax.optimization_barrier((own, *layer))
    left = plane_send(own, "far", 1)
    right = plane_send(own, "far", -1)
    (t_own,) = feed_forward([own], layer)
    left, right, t_own = lax.optimization_barrier((left, right, t_own))
    far = jnp.concatenate([plane_send(left[:2], "far", 1), plane_send(right[2:], "far", -1)])
    t_left, t_right = feed_forward([left, right], layer)
    t_left, t_right, far = lax.optimization_barrier((t_left, t_right, far))
    got = [plane_send(t_right, "far", 1), plane_send(t_left, "far", -1)]
    (t_far,) = feed_forward([far], layer)
    got.append(plane_send(t_far, "far", 2))
    work, operands = inside_scatter
    t_far, *operands = lax.optimization_barrier((t_far, *operands))
    extra = work(*operands)
    *got, extra = lax.optimization_barrier((*got, extra))
    total = t_own.astype(jnp.float32) + sum(g.astype(jnp.float32) for g in got)
    sent = total.astype(jnp.bfloat16)
    parts = [plane_send(sent[1], "near", 2), plane_send(sent[3], "near", 1), plane_send(sent[2], "near", -1)]
    summed = total[0] + sum(p.astype(jnp.float32) for p in parts)
    return (values + summed).astype(jnp.bfloat16), layer, extra


def pack_kernel(*refs):
    out_ref, at = refs[-1], 0
    for ref in refs[:-1]:
        out_ref[:, at : at + ref.shape[-1]] = ref[...].reshape(2, ref.shape[-1])
        at += ref.shape[-1]


def pack(arrays):
    return pl.pallas_call(
        pack_kernel,
        out_shape=jax.ShapeDtypeStruct((2, sum(a.shape[-1] for a in arrays)), jnp.bfloat16),
        compiler_params=pltpu.CompilerParams(vmem_limit_bytes=2 * 1024 * 1024),
    )(*arrays)


def outer_kernel(*refs, spans, share, tile):
    groups, outs = refs[:4], refs[4:]
    step = pl.program_id(0)
    mine = lax.axis_index("pop") * share
    ranks_at = groups[0].shape[1] - 128
    fitness = [(2.0 * g[:, ranks_at : ranks_at + 1].astype(jnp.float32) / 7 - 1.0) / math.sqrt(8) for g in groups]
    for out, (left_at, left_mine, right_at, right_mine) in zip(outs, spans):
        left_cols = pl.ds(pl.multiple_of(left_at + step * tile + (mine if left_mine else 0), 128), tile)
        right_cols = pl.ds(pl.multiple_of(right_at + mine, 128) if right_mine else right_at, out.shape[1])
        total = None
        for group, fit in zip(groups, fitness):
            weighted = (group[:, left_cols].astype(jnp.float32) * fit).T
            right = group[:, right_cols].astype(jnp.float32)
            part = weighted[:, 0:1] * right[0:1] + weighted[:, 1:2] * right[1:2]
            part = part.astype(jnp.bfloat16).astype(jnp.float32)
            total = part if total is None else total + part
        out[...] = total.astype(jnp.bfloat16)


def grouped_outers(groups, spans, share, shape, tile=256):
    rows, cols = shape
    return pl.pallas_call(
        functools.partial(outer_kernel, spans=spans, share=share, tile=tile),
        grid=(rows // tile,),
        in_specs=[pl.BlockSpec(memory_space=pltpu.VMEM)] * 4,
        out_specs=[pl.BlockSpec((tile, cols), lambda i: (i, 0))] * len(spans),
        out_shape=[jax.ShapeDtypeStruct(shape, jnp.bfloat16)] * len(spans),
        compiler_params=pltpu.CompilerParams(vmem_limit_bytes=8 * 1024 * 1024),
        cost_estimate=pl.CostEstimate(flops=UPDATE_FLOPS, bytes_accessed=UPDATE_FLOPS, transcendentals=0),
    )(*groups)


def per_device(hidden_in, norm_gain, w_gate, w_up, w_down, gate_left, gate_right, up_left, up_right, down_left, down_right, ranks):
    members, width = hidden_in.shape[1:]
    section_index = lax.axis_index("pp")
    pops = lax.axis_size("pop")
    vectors = [gate_left[0], gate_right[0], up_left[0], up_right[0], down_left[0], down_right[0]]
    rank_columns = jnp.broadcast_to(ranks.astype(jnp.bfloat16)[:, None], (members, 128))

    def exchange(*arrays):
        packed = pack(arrays)
        return [packed] + [lax.ppermute(packed, "pop", [(i, (i + s) % pops) for i in range(pops)]) for s in (1, 2, 3)]

    lefts = jnp.pad(jnp.concatenate([gate_left[0], up_left[0]]).T, ((0, 0), (0, 124)))
    layer = (w_gate[0], w_up[0], w_down[0], lefts, gate_right[0], up_right[0], down_left[0], down_right[0])

    share, hidden = width // pops, w_gate.shape[-1]
    starts = [0, width, width + hidden, 2 * width + hidden, 2 * (width + hidden), 2 * width + 3 * hidden]
    gl, gr, ul, ur, dl, dr = starts

    def updates(*everyone):
        gate_and_up = grouped_outers(everyone, ((gl, True, gr, False), (ul, True, ur, False)), share, (share, hidden))
        return (*gate_and_up, *grouped_outers(everyone, ((dl, False, dr, True),), share, (hidden, share)))

    first_in = hidden_in.transpose(1, 0, 2)
    first, layer, everyone = section(first_in, norm_gain[0], layer, (exchange, vectors + [rank_columns]), True)
    arrived = lax.ppermute(first, "pp", [(0, 1)])
    second, _, (update_gate, update_up, update_down) = section(arrived, norm_gain[0], layer, (updates, everyone))
    output = jnp.where(section_index == 0, first, second).transpose(1, 0, 2)
    return (output[None], update_gate[None], update_up[None], update_down[None])


def solution(mesh):
    placed = (
        P("tp", "pop", None),
        P("pp", None),
        P("pp", None, "tp"),
        P("pp", None, "tp"),
        P("pp", "tp", None),
        P("pp", "pop", None),
        P("pp", "pop", "tp"),
        P("pp", "pop", None),
        P("pp", "pop", "tp"),
        P("pp", "pop", "tp"),
        P("pp", "pop", None),
        P("pop"),
    )
    return jax.shard_map(
        per_device,
        mesh=mesh,
        in_specs=placed,
        out_specs=(
            P("pp", "tp", "pop", None),
            P("pp", "pop", "tp"),
            P("pp", "pop", "tp"),
            P("pp", "tp", "pop"),
        ),
        check_vma=False,
    )
```

```python
import functools
import math

import jax
import jax.numpy as jnp
from jax import lax
from jax.experimental import pallas as pl
from jax.experimental.pallas import tpu as pltpu
from jax.sharding import PartitionSpec as P

sigma_scale = 0.3
norm_eps = 1e-05
SIDE = 4
UPDATE_FLOPS = 1000
TILE = 256
DOWN_TILE = 1024
FFN_MIB = 16


def plane_route(level, shift):
    pairs = []
    for pop in range(4):
        for z in range(SIDE):
            for x in range(SIDE):
                along_x = (pop % 2 == 0) == (level == "near")
                nz, nx = (z, (x + shift) % SIDE) if along_x else ((z + shift) % SIDE, x)
                pairs.append((pop * 16 + z * SIDE + x, pop * 16 + nz * SIDE + nx))
    return pairs


def plane_send(block, level, shift):
    return lax.ppermute(block, ("pop", "tp"), plane_route(level, shift))


def norm_kernel(block, gain, mark, out):
    values = block[...].astype(jnp.float32)
    mean_sq = jnp.mean(values * values, axis=-1, keepdims=True)
    out[...] = (values * lax.rsqrt(mean_sq + norm_eps) * gain[...]).astype(jnp.bfloat16)


def norm_in_step(block, gain):
    mark = block[0, :, :128]
    route = [(pop * 16 + tp, (pop ^ 1) * 16 + tp) for pop in range(4) for tp in range(16)]
    mark = lax.ppermute(mark, ("pop", "tp"), route)
    return pl.pallas_call(
        norm_kernel,
        in_specs=[pl.BlockSpec(memory_space=pltpu.VMEM)] * 3,
        out_specs=pl.BlockSpec(memory_space=pltpu.VMEM),
        out_shape=jax.ShapeDtypeStruct(block.shape, jnp.bfloat16),
        compiler_params=pltpu.CompilerParams(vmem_limit_bytes=4 * 1024 * 1024),
    )(block, gain.reshape(1, 1, -1), mark)


def ffn_kernel(*refs, blocks):
    pieces, refs = refs[:blocks], refs[blocks:]
    w_gate, w_up, w_down, lefts, gate_right, up_right, down_left, down_right = refs[:8]
    outs, (x_ref, h_ref) = refs[8 : 8 + blocks], refs[8 + blocks :]
    rows = x_ref.shape[0]
    width, hidden = w_gate.shape
    at = 0
    for piece in pieces:
        flat = piece[...].reshape(-1, width)
        x_ref[at : at + flat.shape[0], :] = flat
        at += flat.shape[0]
    member = (lax.broadcasted_iota(jnp.int32, (rows, 1), 0) // 16) % 2
    coef_in = sigma_scale / math.sqrt(width)
    coef_hidden = sigma_scale / math.sqrt(hidden * 16)

    def ranked(sides, at, right, coef):
        first = jnp.where(member == 0, sides[:, at : at + 1] * coef, 0.0)
        second = jnp.where(member == 0, 0.0, sides[:, at + 1 : at + 2] * coef)
        right = right.astype(jnp.float32)
        return first * right[0:1] + second * right[1:2]

    sides = jnp.dot(x_ref[...], lefts[...], preferred_element_type=jnp.float32)
    for step in range(hidden // TILE):
        cols = slice(step * TILE, (step + 1) * TILE)
        gate = jnp.dot(x_ref[...], w_gate[:, cols], preferred_element_type=jnp.float32)
        gate = gate + ranked(sides, 0, gate_right[:, cols], coef_in)
        upper = jnp.dot(x_ref[...], w_up[:, cols], preferred_element_type=jnp.float32)
        upper = upper + ranked(sides, 2, up_right[:, cols], coef_in)
        h_ref[:, cols] = (gate / (1.0 + jnp.exp(-gate)) * upper).astype(jnp.bfloat16)
    across = (((1,), (1,)), ((), ()))
    downs = lax.dot_general(h_ref[...], down_left[...], across, preferred_element_type=jnp.float32)
    for step in range(width // DOWN_TILE):
        cols = slice(step * DOWN_TILE, (step + 1) * DOWN_TILE)
        term = jnp.dot(h_ref[...], w_down[:, cols], preferred_element_type=jnp.float32)
        term = (term + ranked(downs, 0, down_right[:, cols], coef_hidden)).astype(jnp.bfloat16)
        at = 0
        for out in outs:
            size = out.shape[0] * 32
            out[:, :, :, cols] = term[at : at + size].reshape(out.shape[:3] + (DOWN_TILE,))
            at += size


def feed_forward(pieces, layer):
    rows = sum(p.size for p in pieces) // pieces[0].shape[-1]
    width, hidden = layer[0].shape
    vmem = pl.BlockSpec(memory_space=pltpu.VMEM)
    return pl.pallas_call(
        functools.partial(ffn_kernel, blocks=len(pieces)),
        in_specs=[vmem] * (len(pieces) + len(layer)),
        out_specs=[vmem] * len(pieces),
        out_shape=[jax.ShapeDtypeStruct(p.shape, jnp.bfloat16) for p in pieces],
        scratch_shapes=[pltpu.VMEM((rows, width), jnp.bfloat16), pltpu.VMEM((rows, hidden), jnp.bfloat16)],
        compiler_params=pltpu.CompilerParams(vmem_limit_bytes=FFN_MIB * 1024 * 1024),
        cost_estimate=pl.CostEstimate(flops=6 * rows * width * hidden, bytes_accessed=6 * width * hidden, transcendentals=rows * hidden),
    )(*pieces, *layer)


def section(block, gain, layer, inside_scatter, first=False):
    values = block.astype(jnp.float32)
    if first:
        mean_sq = jnp.mean(values * values, axis=-1, keepdims=True)
        normed = (values * lax.rsqrt(mean_sq + norm_eps) * gain).astype(jnp.bfloat16)
    else:
        normed = norm_in_step(block, gain)
    own = jnp.stack([normed] + [plane_send(normed, "near", s) for s in (2, 1, -1)])
    if first:
        own, *layer = lax.optimization_barrier((own, *layer))
    left = plane_send(own, "far", 1)
    right = plane_send(own, "far", -1)
    (t_own,) = feed_forward([own], layer)
    left, right, t_own = lax.optimization_barrier((left, right, t_own))
    far = jnp.concatenate([plane_send(left[:2], "far", 1), plane_send(right[2:], "far", -1)])
    t_left, t_right = feed_forward([left, right], layer)
    t_left, t_right, far = lax.optimization_barrier((t_left, t_right, far))
    got = [plane_send(t_right, "far", 1), plane_send(t_left, "far", -1)]
    (t_far,) = feed_forward([far], layer)
    got.append(plane_send(t_far, "far", 2))
    work, operands = inside_scatter
    t_far, *operands = lax.optimization_barrier((t_far, *operands))
    extra = work(*operands)
    *got, extra = lax.optimization_barrier((*got, extra))
    total = t_own.astype(jnp.float32) + sum(g.astype(jnp.float32) for g in got)
    sent = total.astype(jnp.bfloat16)
    parts = [plane_send(sent[1], "near", 2), plane_send(sent[3], "near", 1), plane_send(sent[2], "near", -1)]
    summed = total[0] + sum(p.astype(jnp.float32) for p in parts)
    return (values + summed).astype(jnp.bfloat16), layer, extra


def pack_kernel(*refs):
    out_ref, at = refs[-1], 0
    for ref in refs[:-1]:
        out_ref[:, at : at + ref.shape[-1]] = ref[...].reshape(2, ref.shape[-1])
        at += ref.shape[-1]


def pack(arrays):
    return pl.pallas_call(
        pack_kernel,
        out_shape=jax.ShapeDtypeStruct((2, sum(a.shape[-1] for a in arrays)), jnp.bfloat16),
        compiler_params=pltpu.CompilerParams(vmem_limit_bytes=2 * 1024 * 1024),
    )(*arrays)


def outer_kernel(*refs, spans, share, tile):
    groups, outs = refs[:4], refs[4:]
    step = pl.program_id(0)
    mine = lax.axis_index("pop") * share
    ranks_at = groups[0].shape[1] - 128
    fitness = [(2.0 * g[:, ranks_at : ranks_at + 1].astype(jnp.float32) / 7 - 1.0) / math.sqrt(8) for g in groups]
    for out, (left_at, left_mine, right_at, right_mine) in zip(outs, spans):
        left_cols = pl.ds(pl.multiple_of(left_at + step * tile + (mine if left_mine else 0), 128), tile)
        right_cols = pl.ds(pl.multiple_of(right_at + mine, 128) if right_mine else right_at, out.shape[1])
        total = None
        for group, fit in zip(groups, fitness):
            weighted = (group[:, left_cols].astype(jnp.float32) * fit).T
            right = group[:, right_cols].astype(jnp.float32)
            part = weighted[:, 0:1] * right[0:1] + weighted[:, 1:2] * right[1:2]
            part = part.astype(jnp.bfloat16).astype(jnp.float32)
            total = part if total is None else total + part
        out[...] = total.astype(jnp.bfloat16)


def grouped_outers(groups, spans, share, shape, tile=256):
    rows, cols = shape
    return pl.pallas_call(
        functools.partial(outer_kernel, spans=spans, share=share, tile=tile),
        grid=(rows // tile,),
        in_specs=[pl.BlockSpec(memory_space=pltpu.VMEM)] * 4,
        out_specs=[pl.BlockSpec((tile, cols), lambda i: (i, 0))] * len(spans),
        out_shape=[jax.ShapeDtypeStruct(shape, jnp.bfloat16)] * len(spans),
        compiler_params=pltpu.CompilerParams(vmem_limit_bytes=8 * 1024 * 1024),
        cost_estimate=pl.CostEstimate(flops=UPDATE_FLOPS, bytes_accessed=UPDATE_FLOPS, transcendentals=0),
    )(*groups)


def per_device(hidden_in, norm_gain, w_gate, w_up, w_down, gate_left, gate_right, up_left, up_right, down_left, down_right, ranks):
    members, width = hidden_in.shape[1:]
    section_index = lax.axis_index("pp")
    pops = lax.axis_size("pop")
    vectors = [gate_left[0], gate_right[0], up_left[0], up_right[0], down_left[0], down_right[0]]
    rank_columns = jnp.broadcast_to(ranks.astype(jnp.bfloat16)[:, None], (members, 128))

    def exchange(*arrays):
        packed = pack(arrays)
        return [packed] + [lax.ppermute(packed, "pop", [(i, (i + s) % pops) for i in range(pops)]) for s in (1, 2, 3)]

    lefts = jnp.pad(jnp.concatenate([gate_left[0], up_left[0]]).T, ((0, 0), (0, 124)))
    layer = (w_gate[0], w_up[0], w_down[0], lefts, gate_right[0], up_right[0], down_left[0], down_right[0])

    share, hidden = width // pops, w_gate.shape[-1]
    starts = [0, width, width + hidden, 2 * width + hidden, 2 * (width + hidden), 2 * width + 3 * hidden]
    gl, gr, ul, ur, dl, dr = starts

    def updates(*everyone):
        gate_and_up = grouped_outers(everyone, ((gl, True, gr, False), (ul, True, ur, False)), share, (share, hidden))
        return (*gate_and_up, *grouped_outers(everyone, ((dl, False, dr, True),), share, (hidden, share)))

    first_in = hidden_in.transpose(1, 0, 2)
    first, layer, everyone = section(first_in, norm_gain[0], layer, (exchange, vectors + [rank_columns]), True)
    arrived = lax.ppermute(first, "pp", [(0, 1)])
    second, _, (update_gate, update_up, update_down) = section(arrived, norm_gain[0], layer, (updates, everyone))
    output = jnp.where(section_index == 0, first, second).transpose(1, 0, 2)
    return (output[None], update_gate[None], update_up[None], update_down[None])


def solution(mesh):
    placed = (
        P("tp", "pop", None),
        P("pp", None),
        P("pp", None, "tp"),
        P("pp", None, "tp"),
        P("pp", "tp", None),
        P("pp", "pop", None),
        P("pp", "pop", "tp"),
        P("pp", "pop", None),
        P("pp", "pop", "tp"),
        P("pp", "pop", "tp"),
        P("pp", "pop", None),
        P("pop"),
    )
    return jax.shard_map(
        per_device,
        mesh=mesh,
        in_specs=placed,
        out_specs=(
            P("pp", "tp", "pop", None),
            P("pp", "pop", "tp"),
            P("pp", "pop", "tp"),
            P("pp", "tp", "pop"),
        ),
        check_vma=False,
    )
```

```python
import functools
import math

import jax
import jax.numpy as jnp
from jax import lax
from jax.experimental import pallas as pl
from jax.experimental.pallas import tpu as pltpu
from jax.sharding import PartitionSpec as P

sigma_scale = 0.3
norm_eps = 1e-05
SIDE = 4
UPDATE_FLOPS = 1000
TILE = 256
DOWN_TILE = 1024
FFN_MIB = 16


def plane_route(level, shift):
    pairs = []
    for pop in range(4):
        for z in range(SIDE):
            for x in range(SIDE):
                along_x = (pop % 2 == 0) == (level == "near")
                nz, nx = (z, (x + shift) % SIDE) if along_x else ((z + shift) % SIDE, x)
                pairs.append((pop * 16 + z * SIDE + x, pop * 16 + nz * SIDE + nx))
    return pairs


def plane_send(block, level, shift):
    return lax.ppermute(block, ("pop", "tp"), plane_route(level, shift))


def norm_kernel(block, gain, mark, out):
    values = block[...].astype(jnp.float32)
    mean_sq = jnp.mean(values * values, axis=-1, keepdims=True)
    out[...] = (values * lax.rsqrt(mean_sq + norm_eps) * gain[...]).astype(jnp.bfloat16)


def other_core(mark):
    route = [(pop * 16 + tp, (pop ^ 1) * 16 + tp) for pop in range(4) for tp in range(16)]
    return lax.ppermute(mark, ("pop", "tp"), route)


def norm_in_step(block, gain):
    mark = other_core(block[0, :, :128])
    return pl.pallas_call(
        norm_kernel,
        in_specs=[pl.BlockSpec(memory_space=pltpu.VMEM)] * 3,
        out_specs=pl.BlockSpec(memory_space=pltpu.VMEM),
        out_shape=jax.ShapeDtypeStruct(block.shape, jnp.bfloat16),
        compiler_params=pltpu.CompilerParams(vmem_limit_bytes=4 * 1024 * 1024),
    )(block, gain.reshape(1, 1, -1), mark)


def ffn_kernel(*refs, blocks, extra):
    pieces, refs = refs[:blocks], refs[blocks:]
    w_gate, w_up, w_down, lefts, gate_right, up_right, down_left, down_right = refs[:8]
    outs, (x_ref, h_ref) = refs[8 + extra : 8 + extra + blocks], refs[8 + extra + blocks :]
    rows = x_ref.shape[0]
    width, hidden = w_gate.shape
    at = 0
    for piece in pieces:
        flat = piece[...].reshape(-1, width)
        x_ref[at : at + flat.shape[0], :] = flat
        at += flat.shape[0]
    member = (lax.broadcasted_iota(jnp.int32, (rows, 1), 0) // 16) % 2
    coef_in = sigma_scale / math.sqrt(width)
    coef_hidden = sigma_scale / math.sqrt(hidden * 16)

    def ranked(sides, at, right, coef):
        first = jnp.where(member == 0, sides[:, at : at + 1] * coef, 0.0)
        second = jnp.where(member == 0, 0.0, sides[:, at + 1 : at + 2] * coef)
        right = right.astype(jnp.float32)
        return first * right[0:1] + second * right[1:2]

    sides = jnp.dot(x_ref[...], lefts[...], preferred_element_type=jnp.float32)
    for step in range(hidden // TILE):
        cols = slice(step * TILE, (step + 1) * TILE)
        gate = jnp.dot(x_ref[...], w_gate[:, cols], preferred_element_type=jnp.float32)
        gate = gate + ranked(sides, 0, gate_right[:, cols], coef_in)
        upper = jnp.dot(x_ref[...], w_up[:, cols], preferred_element_type=jnp.float32)
        upper = upper + ranked(sides, 2, up_right[:, cols], coef_in)
        h_ref[:, cols] = (gate / (1.0 + jnp.exp(-gate)) * upper).astype(jnp.bfloat16)
    across = (((1,), (1,)), ((), ()))
    downs = lax.dot_general(h_ref[...], down_left[...], across, preferred_element_type=jnp.float32)
    for step in range(width // DOWN_TILE):
        cols = slice(step * DOWN_TILE, (step + 1) * DOWN_TILE)
        term = jnp.dot(h_ref[...], w_down[:, cols], preferred_element_type=jnp.float32)
        term = (term + ranked(downs, 0, down_right[:, cols], coef_hidden)).astype(jnp.bfloat16)
        at = 0
        for out in outs:
            size = out.shape[0] * 32
            out[:, :, :, cols] = term[at : at + size].reshape(out.shape[:3] + (DOWN_TILE,))
            at += size


def feed_forward(pieces, layer):
    rows = sum(p.size for p in pieces) // pieces[0].shape[-1]
    width, hidden = layer[0].shape
    vmem = pl.BlockSpec(memory_space=pltpu.VMEM)
    return pl.pallas_call(
        functools.partial(ffn_kernel, blocks=len(pieces), extra=len(layer) - 8),
        in_specs=[vmem] * (len(pieces) + len(layer)),
        out_specs=[vmem] * len(pieces),
        out_shape=[jax.ShapeDtypeStruct(p.shape, jnp.bfloat16) for p in pieces],
        scratch_shapes=[pltpu.VMEM((rows, width), jnp.bfloat16), pltpu.VMEM((rows, hidden), jnp.bfloat16)],
        compiler_params=pltpu.CompilerParams(vmem_limit_bytes=FFN_MIB * 1024 * 1024),
        cost_estimate=pl.CostEstimate(flops=6 * rows * width * hidden, bytes_accessed=6 * width * hidden, transcendentals=rows * hidden),
    )(*pieces, *layer)


def section(block, gain, layer, inside_scatter, first=False):
    values = block.astype(jnp.float32)
    if first:
        mean_sq = jnp.mean(values * values, axis=-1, keepdims=True)
        normed = (values * lax.rsqrt(mean_sq + norm_eps) * gain).astype(jnp.bfloat16)
    else:
        normed = norm_in_step(block, gain)
    own = jnp.stack([normed] + [plane_send(normed, "near", s) for s in (2, 1, -1)])
    if first:
        own, *layer = lax.optimization_barrier((own, *layer))
    left = plane_send(own, "far", 1)
    right = plane_send(own, "far", -1)
    (t_own,) = feed_forward([own], layer)
    left, right, t_own = lax.optimization_barrier((left, right, t_own))
    far = jnp.concatenate([plane_send(left[:2], "far", 1), plane_send(right[2:], "far", -1)])
    t_left, t_right = feed_forward([left, right], layer)
    t_left, t_right, far = lax.optimization_barrier((t_left, t_right, far))
    got = [plane_send(t_right, "far", 1), plane_send(t_left, "far", -1)]
    (t_far,) = feed_forward([far], (*layer, other_core(t_left[0, 0, :, :128])))
    got.append(plane_send(t_far, "far", 2))
    work, operands = inside_scatter
    t_far, *operands = lax.optimization_barrier((t_far, *operands))
    extra = work(*operands)
    *got, extra = lax.optimization_barrier((*got, extra))
    total = t_own.astype(jnp.float32) + sum(g.astype(jnp.float32) for g in got)
    sent = total.astype(jnp.bfloat16)
    parts = [plane_send(sent[1], "near", 2), plane_send(sent[3], "near", 1), plane_send(sent[2], "near", -1)]
    summed = total[0] + sum(p.astype(jnp.float32) for p in parts)
    return (values + summed).astype(jnp.bfloat16), layer, extra


def pack_kernel(*refs):
    out_ref, at = refs[-1], 0
    for ref in refs[:-1]:
        out_ref[:, at : at + ref.shape[-1]] = ref[...].reshape(2, ref.shape[-1])
        at += ref.shape[-1]


def pack(arrays):
    return pl.pallas_call(
        pack_kernel,
        out_shape=jax.ShapeDtypeStruct((2, sum(a.shape[-1] for a in arrays)), jnp.bfloat16),
        compiler_params=pltpu.CompilerParams(vmem_limit_bytes=2 * 1024 * 1024),
    )(*arrays)


def outer_kernel(*refs, spans, share, tile):
    groups, outs = refs[:4], refs[4:]
    step = pl.program_id(0)
    mine = lax.axis_index("pop") * share
    ranks_at = groups[0].shape[1] - 128
    fitness = [(2.0 * g[:, ranks_at : ranks_at + 1].astype(jnp.float32) / 7 - 1.0) / math.sqrt(8) for g in groups]
    for out, (left_at, left_mine, right_at, right_mine) in zip(outs, spans):
        left_cols = pl.ds(pl.multiple_of(left_at + step * tile + (mine if left_mine else 0), 128), tile)
        right_cols = pl.ds(pl.multiple_of(right_at + mine, 128) if right_mine else right_at, out.shape[1])
        total = None
        for group, fit in zip(groups, fitness):
            weighted = (group[:, left_cols].astype(jnp.float32) * fit).T
            right = group[:, right_cols].astype(jnp.float32)
            part = weighted[:, 0:1] * right[0:1] + weighted[:, 1:2] * right[1:2]
            part = part.astype(jnp.bfloat16).astype(jnp.float32)
            total = part if total is None else total + part
        out[...] = total.astype(jnp.bfloat16)


def grouped_outers(groups, spans, share, shape, tile=256):
    rows, cols = shape
    return pl.pallas_call(
        functools.partial(outer_kernel, spans=spans, share=share, tile=tile),
        grid=(rows // tile,),
        in_specs=[pl.BlockSpec(memory_space=pltpu.VMEM)] * 4,
        out_specs=[pl.BlockSpec((tile, cols), lambda i: (i, 0))] * len(spans),
        out_shape=[jax.ShapeDtypeStruct(shape, jnp.bfloat16)] * len(spans),
        compiler_params=pltpu.CompilerParams(vmem_limit_bytes=8 * 1024 * 1024),
        cost_estimate=pl.CostEstimate(flops=UPDATE_FLOPS, bytes_accessed=UPDATE_FLOPS, transcendentals=0),
    )(*groups)


def per_device(hidden_in, norm_gain, w_gate, w_up, w_down, gate_left, gate_right, up_left, up_right, down_left, down_right, ranks):
    members, width = hidden_in.shape[1:]
    section_index = lax.axis_index("pp")
    pops = lax.axis_size("pop")
    vectors = [gate_left[0], gate_right[0], up_left[0], up_right[0], down_left[0], down_right[0]]
    rank_columns = jnp.broadcast_to(ranks.astype(jnp.bfloat16)[:, None], (members, 128))

    def exchange(*arrays):
        packed = pack(arrays)
        return [packed] + [lax.ppermute(packed, "pop", [(i, (i + s) % pops) for i in range(pops)]) for s in (1, 2, 3)]

    lefts = jnp.pad(jnp.concatenate([gate_left[0], up_left[0]]).T, ((0, 0), (0, 124)))
    layer = (w_gate[0], w_up[0], w_down[0], lefts, gate_right[0], up_right[0], down_left[0], down_right[0])

    share, hidden = width // pops, w_gate.shape[-1]
    starts = [0, width, width + hidden, 2 * width + hidden, 2 * (width + hidden), 2 * width + 3 * hidden]
    gl, gr, ul, ur, dl, dr = starts

    def updates(*everyone):
        gate_and_up = grouped_outers(everyone, ((gl, True, gr, False), (ul, True, ur, False)), share, (share, hidden))
        return (*gate_and_up, *grouped_outers(everyone, ((dl, False, dr, True),), share, (hidden, share)))

    first_in = hidden_in.transpose(1, 0, 2)
    first, layer, everyone = section(first_in, norm_gain[0], layer, (exchange, vectors + [rank_columns]), True)
    arrived = lax.ppermute(first, "pp", [(0, 1)])
    second, _, (update_gate, update_up, update_down) = section(arrived, norm_gain[0], layer, (updates, everyone))
    output = jnp.where(section_index == 0, first, second).transpose(1, 0, 2)
    return (output[None], update_gate[None], update_up[None], update_down[None])


def solution(mesh):
    placed = (
        P("tp", "pop", None),
        P("pp", None),
        P("pp", None, "tp"),
        P("pp", None, "tp"),
        P("pp", "tp", None),
        P("pp", "pop", None),
        P("pp", "pop", "tp"),
        P("pp", "pop", None),
        P("pp", "pop", "tp"),
        P("pp", "pop", "tp"),
        P("pp", "pop", None),
        P("pop"),
    )
    return jax.shard_map(
        per_device,
        mesh=mesh,
        in_specs=placed,
        out_specs=(
            P("pp", "tp", "pop", None),
            P("pp", "pop", "tp"),
            P("pp", "pop", "tp"),
            P("pp", "tp", "pop"),
        ),
        check_vma=False,
    )
```

```python
import functools
import math

import jax
import jax.numpy as jnp
from jax import lax
from jax.experimental import pallas as pl
from jax.experimental.pallas import tpu as pltpu
from jax.sharding import PartitionSpec as P

sigma_scale = 0.3
norm_eps = 1e-05
SIDE = 4
UPDATE_FLOPS = 1000
TILE = 256
DOWN_TILE = 1024
FFN_MIB = 16


def plane_route(level, shift):
    pairs = []
    for pop in range(4):
        for z in range(SIDE):
            for x in range(SIDE):
                along_x = (pop % 2 == 0) == (level == "near")
                nz, nx = (z, (x + shift) % SIDE) if along_x else ((z + shift) % SIDE, x)
                pairs.append((pop * 16 + z * SIDE + x, pop * 16 + nz * SIDE + nx))
    return pairs


def plane_send(block, level, shift):
    return lax.ppermute(block, ("pop", "tp"), plane_route(level, shift))


def norm_kernel(block, gain, mark, out):
    values = block[...].astype(jnp.float32)
    mean_sq = jnp.mean(values * values, axis=-1, keepdims=True)
    out[...] = (values * lax.rsqrt(mean_sq + norm_eps) * gain[...]).astype(jnp.bfloat16)


def first_norm_kernel(block, gain, out):
    for member in range(out.shape[0]):
        values = block[:, member, :].astype(jnp.float32)
        mean_sq = jnp.mean(values * values, axis=-1, keepdims=True)
        out[member] = (values * lax.rsqrt(mean_sq + norm_eps) * gain[...]).astype(jnp.bfloat16)


def first_norm(block, gain):
    tokens, members, width = block.shape
    return pl.pallas_call(
        first_norm_kernel,
        in_specs=[pl.BlockSpec(memory_space=pltpu.VMEM)] * 2,
        out_specs=pl.BlockSpec(memory_space=pltpu.VMEM),
        out_shape=jax.ShapeDtypeStruct((members, tokens, width), jnp.bfloat16),
        compiler_params=pltpu.CompilerParams(vmem_limit_bytes=4 * 1024 * 1024),
    )(block, gain.reshape(1, -1))


def other_core(mark):
    route = [(pop * 16 + tp, (pop ^ 1) * 16 + tp) for pop in range(4) for tp in range(16)]
    return lax.ppermute(mark, ("pop", "tp"), route)


def norm_in_step(block, gain):
    mark = other_core(block[0, :, :128])
    return pl.pallas_call(
        norm_kernel,
        in_specs=[pl.BlockSpec(memory_space=pltpu.VMEM)] * 3,
        out_specs=pl.BlockSpec(memory_space=pltpu.VMEM),
        out_shape=jax.ShapeDtypeStruct(block.shape, jnp.bfloat16),
        compiler_params=pltpu.CompilerParams(vmem_limit_bytes=4 * 1024 * 1024),
    )(block, gain.reshape(1, 1, -1), mark)


def ffn_kernel(*refs, blocks, extra):
    pieces, refs = refs[:blocks], refs[blocks:]
    w_gate, w_up, w_down, lefts, gate_right, up_right, down_left, down_right = refs[:8]
    outs, (x_ref, h_ref) = refs[8 + extra : 8 + extra + blocks], refs[8 + extra + blocks :]
    rows = x_ref.shape[0]
    width, hidden = w_gate.shape
    at = 0
    for piece in pieces:
        flat = piece[...].reshape(-1, width)
        x_ref[at : at + flat.shape[0], :] = flat
        at += flat.shape[0]
    member = (lax.broadcasted_iota(jnp.int32, (rows, 1), 0) // 16) % 2
    coef_in = sigma_scale / math.sqrt(width)
    coef_hidden = sigma_scale / math.sqrt(hidden * 16)

    def ranked(sides, at, right, coef):
        first = jnp.where(member == 0, sides[:, at : at + 1] * coef, 0.0)
        second = jnp.where(member == 0, 0.0, sides[:, at + 1 : at + 2] * coef)
        right = right.astype(jnp.float32)
        return first * right[0:1] + second * right[1:2]

    sides = jnp.dot(x_ref[...], lefts[...], preferred_element_type=jnp.float32)
    for step in range(hidden // TILE):
        cols = slice(step * TILE, (step + 1) * TILE)
        gate = jnp.dot(x_ref[...], w_gate[:, cols], preferred_element_type=jnp.float32)
        gate = gate + ranked(sides, 0, gate_right[:, cols], coef_in)
        upper = jnp.dot(x_ref[...], w_up[:, cols], preferred_element_type=jnp.float32)
        upper = upper + ranked(sides, 2, up_right[:, cols], coef_in)
        h_ref[:, cols] = (gate / (1.0 + jnp.exp(-gate)) * upper).astype(jnp.bfloat16)
    across = (((1,), (1,)), ((), ()))
    downs = lax.dot_general(h_ref[...], down_left[...], across, preferred_element_type=jnp.float32)
    for step in range(width // DOWN_TILE):
        cols = slice(step * DOWN_TILE, (step + 1) * DOWN_TILE)
        term = jnp.dot(h_ref[...], w_down[:, cols], preferred_element_type=jnp.float32)
        term = (term + ranked(downs, 0, down_right[:, cols], coef_hidden)).astype(jnp.bfloat16)
        at = 0
        for out in outs:
            size = out.shape[0] * 32
            out[:, :, :, cols] = term[at : at + size].reshape(out.shape[:3] + (DOWN_TILE,))
            at += size


def feed_forward(pieces, layer):
    rows = sum(p.size for p in pieces) // pieces[0].shape[-1]
    width, hidden = layer[0].shape
    vmem = pl.BlockSpec(memory_space=pltpu.VMEM)
    return pl.pallas_call(
        functools.partial(ffn_kernel, blocks=len(pieces), extra=len(layer) - 8),
        in_specs=[vmem] * (len(pieces) + len(layer)),
        out_specs=[vmem] * len(pieces),
        out_shape=[jax.ShapeDtypeStruct(p.shape, jnp.bfloat16) for p in pieces],
        scratch_shapes=[pltpu.VMEM((rows, width), jnp.bfloat16), pltpu.VMEM((rows, hidden), jnp.bfloat16)],
        compiler_params=pltpu.CompilerParams(vmem_limit_bytes=FFN_MIB * 1024 * 1024),
        cost_estimate=pl.CostEstimate(flops=6 * rows * width * hidden, bytes_accessed=6 * width * hidden, transcendentals=rows * hidden),
    )(*pieces, *layer)


def section(block, gain, layer, inside_scatter, tokens_first=None):
    first = tokens_first is not None
    values = block.astype(jnp.float32)
    if first:
        normed = first_norm(tokens_first, gain)
    else:
        normed = norm_in_step(block, gain)
    own = jnp.stack([normed] + [plane_send(normed, "near", s) for s in (2, 1, -1)])
    if first:
        own, *layer = lax.optimization_barrier((own, *layer))
    left = plane_send(own, "far", 1)
    right = plane_send(own, "far", -1)
    (t_own,) = feed_forward([own], layer)
    left, right, t_own = lax.optimization_barrier((left, right, t_own))
    far = jnp.concatenate([plane_send(left[:2], "far", 1), plane_send(right[2:], "far", -1)])
    t_left, t_right = feed_forward([left, right], layer)
    t_left, t_right, far = lax.optimization_barrier((t_left, t_right, far))
    got = [plane_send(t_right, "far", 1), plane_send(t_left, "far", -1)]
    (t_far,) = feed_forward([far], (*layer, other_core(t_left[0, 0, :, :128])))
    got.append(plane_send(t_far, "far", 2))
    work, operands = inside_scatter
    t_far, *operands = lax.optimization_barrier((t_far, *operands))
    extra = work(*operands)
    *got, extra = lax.optimization_barrier((*got, extra))
    total = t_own.astype(jnp.float32) + sum(g.astype(jnp.float32) for g in got)
    sent = total.astype(jnp.bfloat16)
    parts = [plane_send(sent[1], "near", 2), plane_send(sent[3], "near", 1), plane_send(sent[2], "near", -1)]
    summed = total[0] + sum(p.astype(jnp.float32) for p in parts)
    return (values + summed).astype(jnp.bfloat16), layer, extra


def pack_kernel(*refs):
    out_ref, at = refs[-1], 0
    for ref in refs[:-1]:
        out_ref[:, at : at + ref.shape[-1]] = ref[...].reshape(2, ref.shape[-1])
        at += ref.shape[-1]


def pack(arrays):
    return pl.pallas_call(
        pack_kernel,
        out_shape=jax.ShapeDtypeStruct((2, sum(a.shape[-1] for a in arrays)), jnp.bfloat16),
        compiler_params=pltpu.CompilerParams(vmem_limit_bytes=2 * 1024 * 1024),
    )(*arrays)


def outer_kernel(*refs, spans, share, tile):
    groups, outs = refs[:4], refs[4:]
    step = pl.program_id(0)
    mine = lax.axis_index("pop") * share
    ranks_at = groups[0].shape[1] - 128
    fitness = [(2.0 * g[:, ranks_at : ranks_at + 1].astype(jnp.float32) / 7 - 1.0) / math.sqrt(8) for g in groups]
    for out, (left_at, left_mine, right_at, right_mine) in zip(outs, spans):
        left_cols = pl.ds(pl.multiple_of(left_at + step * tile + (mine if left_mine else 0), 128), tile)
        right_cols = pl.ds(pl.multiple_of(right_at + mine, 128) if right_mine else right_at, out.shape[1])
        total = None
        for group, fit in zip(groups, fitness):
            weighted = (group[:, left_cols].astype(jnp.float32) * fit).T
            right = group[:, right_cols].astype(jnp.float32)
            part = weighted[:, 0:1] * right[0:1] + weighted[:, 1:2] * right[1:2]
            part = part.astype(jnp.bfloat16).astype(jnp.float32)
            total = part if total is None else total + part
        out[...] = total.astype(jnp.bfloat16)


def grouped_outers(groups, spans, share, shape, tile=256):
    rows, cols = shape
    return pl.pallas_call(
        functools.partial(outer_kernel, spans=spans, share=share, tile=tile),
        grid=(rows // tile,),
        in_specs=[pl.BlockSpec(memory_space=pltpu.VMEM)] * 4,
        out_specs=[pl.BlockSpec((tile, cols), lambda i: (i, 0))] * len(spans),
        out_shape=[jax.ShapeDtypeStruct(shape, jnp.bfloat16)] * len(spans),
        compiler_params=pltpu.CompilerParams(vmem_limit_bytes=8 * 1024 * 1024),
        cost_estimate=pl.CostEstimate(flops=UPDATE_FLOPS, bytes_accessed=UPDATE_FLOPS, transcendentals=0),
    )(*groups)


def per_device(hidden_in, norm_gain, w_gate, w_up, w_down, gate_left, gate_right, up_left, up_right, down_left, down_right, ranks):
    members, width = hidden_in.shape[1:]
    section_index = lax.axis_index("pp")
    pops = lax.axis_size("pop")
    vectors = [gate_left[0], gate_right[0], up_left[0], up_right[0], down_left[0], down_right[0]]
    rank_columns = jnp.broadcast_to(ranks.astype(jnp.bfloat16)[:, None], (members, 128))

    def exchange(*arrays):
        packed = pack(arrays)
        return [packed] + [lax.ppermute(packed, "pop", [(i, (i + s) % pops) for i in range(pops)]) for s in (1, 2, 3)]

    lefts = jnp.pad(jnp.concatenate([gate_left[0], up_left[0]]).T, ((0, 0), (0, 124)))
    layer = (w_gate[0], w_up[0], w_down[0], lefts, gate_right[0], up_right[0], down_left[0], down_right[0])

    share, hidden = width // pops, w_gate.shape[-1]
    starts = [0, width, width + hidden, 2 * width + hidden, 2 * (width + hidden), 2 * width + 3 * hidden]
    gl, gr, ul, ur, dl, dr = starts

    def updates(*everyone):
        gate_and_up = grouped_outers(everyone, ((gl, True, gr, False), (ul, True, ur, False)), share, (share, hidden))
        return (*gate_and_up, *grouped_outers(everyone, ((dl, False, dr, True),), share, (hidden, share)))

    first_in = hidden_in.transpose(1, 0, 2)
    first, layer, everyone = section(first_in, norm_gain[0], layer, (exchange, vectors + [rank_columns]), hidden_in)
    arrived = lax.ppermute(first, "pp", [(0, 1)])
    second, _, (update_gate, update_up, update_down) = section(arrived, norm_gain[0], layer, (updates, everyone))
    output = jnp.where(section_index == 0, first, second).transpose(1, 0, 2)
    return (output[None], update_gate[None], update_up[None], update_down[None])


def solution(mesh):
    placed = (
        P("tp", "pop", None),
        P("pp", None),
        P("pp", None, "tp"),
        P("pp", None, "tp"),
        P("pp", "tp", None),
        P("pp", "pop", None),
        P("pp", "pop", "tp"),
        P("pp", "pop", None),
        P("pp", "pop", "tp"),
        P("pp", "pop", "tp"),
        P("pp", "pop", None),
        P("pop"),
    )
    return jax.shard_map(
        per_device,
        mesh=mesh,
        in_specs=placed,
        out_specs=(
            P("pp", "tp", "pop", None),
            P("pp", "pop", "tp"),
            P("pp", "pop", "tp"),
            P("pp", "tp", "pop"),
        ),
        check_vma=False,
    )
```
